32 devices in a mesh: grp: 2 (over y), gx: 4 (over z), trc: 2 (over x), gy: 2 (over core).
Axes of the slice: x: 2, y: 2, z: 4, core: 2. Of those that a mesh axis runs over, the one named last changes fastest.
Arguments:
- tracers: float32 [16, 8, 180, 256], P(('grp', 'trc'), None, 'gx', 'gy'), parts along dimension 0, may hold values from -6 to 6
- colors: int32 [8, 180, 256], P(None, 'gx', 'gy'), may hold values from 0 to 7
- land_mask: int32 [8, 180, 256], P('trc', 'gx', 'gy'), may hold values 0 or 1
- east_velocity: float32 [8, 180, 256], P('trc', 'gx', 'gy'), may hold values from -2 to 2
- north_velocity: float32 [8, 180, 256], P('trc', 'gx', 'gy'), may hold values from -2 to 2
- mixing: float32 [8, 180, 256], P('trc', 'gx', 'gy'), may hold values from 0.01 to 0.1
- slope_east: float32 [8, 180, 256], P('trc', 'gx', 'gy'), may hold values from -2.5 to 2.5
- slope_north: float32 [8, 180, 256], P('trc', 'gx', 'gy'), may hold values from -2.5 to 2.5
Outputs:
- advanced: float32 [16, 8, 180, 256], P(('grp', 'trc'), None, 'gx', 'gy'), parts along dimension 0
The draws below stay inside these ranges and needn't reach their ends.
There are 2 independent parts, one for each index of `grp`. The reference program is written for one: setup_inputs(seed, part) draws one part's arguments, and reference() takes and returns one part's arrays. A program takes and returns all parts, laid end to end along the dimension named above; an argument that names none is the same for every part. Nothing has to cross between parts.
Inputs may be any that keep to these rules, and one draw needn't show every extreme that they name: colors name tracers of one batch.
All inputs are finite; a program needn't handle non-finite values. No bound on the sum of `land_mask` on one device may be relied on, other than what follows from the above.
Results may differ from the reference program's by a relative error of at most 0.0003.
Values sent between devices are 32-bit elements; how exact they have to be, the bound alone decides.
A program may use at most 64 MiB of HBM per device.

```python
import math
import jax
import jax.numpy as jnp
from jax import lax

K = 8
SUBSTEPS = 4
NX = 180
NY = 256
NT = 8


def with_ends(values, key, low, largest):
    dims = values.shape
    spot = [jax.random.randint(jax.random.fold_in(key, axis), (), 0, dims[axis]) for axis in range(len(dims))]
    values = values.at[tuple(spot)].set(low)
    longest = dims.index(max(dims))
    spot[longest] = (spot[longest] + 1) % dims[longest]
    return values.at[tuple(spot)].set(largest)


def level_of(rng, dims, cuts, least, high):
    factor_of, own = 1.0, jax.random.fold_in(rng, 6)
    for axis_at, parts in cuts:
        steps = jnp.exp(jax.random.uniform(jax.random.fold_in(own, axis_at), (parts,), jnp.float32, least / len(cuts), high / len(cuts)))
        factor_of = factor_of * jnp.repeat(steps, dims[axis_at] // parts).reshape([-1 if axis == axis_at else 1 for axis in range(len(dims))])
    return factor_of


def centred(own_key, extent, deviation, most, split=(), kind=jnp.bfloat16):
    gain = level_of(own_key, extent, split, -0.22, 0.18) if split else 1.0
    entries = jax.random.normal(own_key, extent, jnp.float32) * deviation * gain
    return jnp.minimum(jnp.maximum(entries, -most), most).astype(kind)


def setup_inputs(seed: int = 0, part: int = 0) -> dict:
    seeds = jax.random.split(jax.random.key(seed), 9)
    part_splits = jax.random.split(jax.random.fold_in(seeds[8], part), 9)
    return {
        "tracers": centred(part_splits[0], (NT, K, NX, NY), 1.0, 6.0, ((0, 2), (2, 4), (3, 2)), jnp.float32),
        "colors": with_ends(jax.random.randint(seeds[1], (K, NX, NY), 0, NT), jax.random.fold_in(seeds[1], 1), 0, NT - 1).astype(jnp.int32),
        "land_mask": with_ends((jax.random.randint(seeds[2], (K, NX, NY), 0, 10) < 9).astype(jnp.int32), jax.random.fold_in(seeds[2], 1), 0, 1),
        "east_velocity": centred(seeds[3], (K, NX, NY), 0.15, 2.0, ((0, 2), (1, 4), (2, 2)), jnp.float32),
        "north_velocity": centred(seeds[4], (K, NX, NY), 0.15, 2.0, ((0, 2), (1, 4), (2, 2)), jnp.float32),
        "mixing": jnp.clip(jnp.exp(math.log(0.1) - 2.3025851 * jax.random.uniform(seeds[5], (K, NX, NY), jnp.float32) ** level_of(seeds[5], (K, NX, NY), ((0, 2), (1, 4), (2, 2)), -0.2, 0.2)), 0.01, 0.1),
        "slope_east": centred(seeds[6], (K, NX, NY), 0.5, 2.5, ((0, 2), (1, 4), (2, 2)), jnp.float32),
        "slope_north": centred(seeds[7], (K, NX, NY), 0.5, 2.5, ((0, 2), (1, 4), (2, 2)), jnp.float32),
    }


time_step = 0.8
pulse_height = 1.0


def vertical(field):
    padded = jnp.pad(field, ((1, 1), (0, 0), (0, 0)))
    return 0.5 * (padded[2:] - padded[:-2])


def northward(field):
    return jnp.concatenate([field[:, :, 1:], field[:, ::-1, -1:]], axis=2)


def reference(tracers, colors, land_mask, east_velocity, north_velocity, mixing, slope_east, slope_north):
    wet_mask = land_mask.astype(jnp.float32)
    wet_east = jnp.roll(wet_mask, -1, axis=1)
    wet_north = jnp.concatenate([wet_mask[:, :, 1:], jnp.ones_like(wet_mask[:, :, :1])], axis=2)
    open_east = wet_mask * wet_east
    open_north = wet_mask * wet_north

    def advance(inputs):
        field, label = inputs
        field = field + pulse_height * jnp.where(colors == label, wet_mask, jnp.float32(0.0))
        for substep in range(SUBSTEPS):
            field_east = jnp.roll(field, -1, axis=1)
            field_north = northward(field)
            slope_here = vertical(field)
            slope_eastern = jnp.roll(slope_here, -1, axis=1)
            slope_northern = northward(slope_here)
            flux_east = (jnp.maximum(east_velocity, 0.0) * field + jnp.minimum(east_velocity, 0.0) * field_east
                         - mixing * (field_east - field)
                         - mixing * slope_east * (0.5 * (slope_here + slope_eastern))) * open_east
            flux_north = (jnp.maximum(north_velocity, 0.0) * field + jnp.minimum(north_velocity, 0.0) * field_north
                          - mixing * (field_north - field)
                          - mixing * slope_north * (0.5 * (slope_here + slope_northern))) * open_north
            flux_west = jnp.roll(flux_east, 1, axis=1)
            flux_south = jnp.concatenate([jnp.zeros_like(flux_north[:, :, :1]), flux_north[:, :, :-1]], axis=2)
            field = field - time_step * (wet_mask * ((flux_east - flux_west) + (flux_north - flux_south)))
        return field

    labels = jnp.arange(tracers.shape[0], dtype=jnp.int32)
    return lax.map(advance, (tracers, labels))
```

```python
import functools

import jax
import jax.numpy as jnp
from jax import lax
from jax.experimental import pallas as pl
from jax.experimental.pallas import tpu as pltpu
from jax.sharding import PartitionSpec as P

SUBSTEPS = 4
time_step = 0.8
pulse_height = 1.0
MESH = pl.DeviceIdType.MESH
OFF = 8


def tile_starts(columns):
    half = -(-columns // 16)
    return [8 * a for a in range(half)] + [columns - 8 - 8 * a for a in reversed(range(half))]


def kernel(
    n_trc, n_gx, tr, col, mask, u_in, v_in, m_in, se_in, sn_in, out,
    ph, mk, west_edge, east_edge, side, west_land, east_land, side_land,
    coef, fx, row_send, lane_send, row_land, lane_land, halo,
    own_sem, gs_sem, gr_sem, es_sem, er_sem, hs_sem, hr_sem,
):
    tracers, levels, columns, lanes = tr.shape
    own = mask.shape[0]
    starts = tile_starts(columns)
    tiles = len(starts)
    me, gx, gy = lax.axis_index("trc"), lax.axis_index("gx"), lax.axis_index("gy")
    east = lax.rem(gx + 1, n_gx)
    west = lax.rem(gx + n_gx - 1, n_gx)
    other, mirror = 1 - gy, n_gx - 1 - gx
    top = gy == 1
    lane = lax.broadcasted_iota(jnp.int32, (8, lanes), 1)
    row = lax.broadcasted_iota(jnp.int32, (8, lanes), 0)
    top_f = jnp.full((8, lanes), gy, jnp.int32).astype(jnp.float32)
    is_top = jnp.full((8, lanes), gy, jnp.int32) == 1

    barrier = pltpu.get_barrier_semaphore()
    for d in range(n_trc):
        p = lax.rem(me + d, n_trc)
        if d:
            pl.semaphore_signal(barrier, inc=1, device_id={"trc": p}, device_id_type=MESH)
        for where in ({"trc": p, "gx": east}, {"trc": p, "gx": west}, {"trc": p, "gy": other}):
            pl.semaphore_signal(barrier, inc=1, device_id=where, device_id_type=MESH)
    pl.semaphore_signal(barrier, inc=1, device_id={"gx": mirror}, device_id_type=MESH)
    pl.semaphore_wait(barrier, 4 * n_trc)

    mine = pl.ds(me * own, own)
    blocks = [(mask, mk.at[mine])] + [
        (ref, ph.at[f, mine]) for f, ref in enumerate((u_in, v_in, m_in, se_in, sn_in))
    ]
    gathers, locals_ = [], []
    for f, (src, dst) in enumerate(blocks):
        for d in range(1, n_trc):
            copy = pltpu.make_async_remote_copy(
                src_ref=src, dst_ref=dst, send_sem=gs_sem.at[f, d], recv_sem=gr_sem.at[f, d],
                device_id={"trc": lax.rem(me + d, n_trc)}, device_id_type=MESH,
            )
            copy.start()
            gathers.append(copy)
        copy = pltpu.make_async_copy(src, dst, own_sem.at[f])
        copy.start()
        locals_.append(copy)

    west_edge[...] = jnp.zeros_like(west_edge)
    east_edge[...] = jnp.zeros_like(east_edge)
    for l in range(own):
        for f, ref in enumerate((u_in, m_in, se_in)):
            west_edge[f, l : l + 1, :] = ref[l, columns - 1 : columns, :]
        west_edge[3, l : l + 1, :] = mask[l, columns - 1 : columns, :].astype(jnp.float32)
        east_edge[l : l + 1, :] = mask[l, 0:1, :].astype(jnp.float32)
    for r, start in enumerate(starts):
        acc = jnp.zeros((8, lanes), jnp.float32)
        for f, ref in enumerate((v_in, m_in, sn_in, mask)):
            for l in range(own):
                x = f * own + l
                value = ref[l, start : start + 8, :].astype(jnp.float32)
                acc = jnp.where(lane // 2 == x, pltpu.roll(value, 2 * x + 1, 1), acc)
        side[r] = acc
    edges = []
    for d in range(n_trc):
        p = lax.rem(me + d, n_trc)
        for e, (src, dst, where) in enumerate((
            (west_edge, west_land.at[me], {"trc": p, "gx": east}),
            (east_edge, east_land.at[me], {"trc": p, "gx": west}),
            (side, side_land.at[me], {"trc": p, "gy": other}),
        )):
            copy = pltpu.make_async_remote_copy(
                src_ref=src, dst_ref=dst, send_sem=es_sem.at[e, d], recv_sem=er_sem.at[e, d],
                device_id=where, device_id_type=MESH,
            )
            copy.start()
            edges.append(copy)

    def halo_copies(slot, t):
        def remote(src, dst, e, where):
            return pltpu.make_async_remote_copy(
                src_ref=src, dst_ref=dst, send_sem=hs_sem.at[e, t], recv_sem=hr_sem.at[e, slot, t],
                device_id=where, device_id_type=MESH,
            )

        return (
            remote(row_send.at[0, t], row_land.at[0, slot, t], 0, {"gx": west}),
            remote(row_send.at[1, t], row_land.at[1, slot, t], 1, {"gx": east}),
            remote(lane_send.at[t], lane_land.at[0, slot, t], 2, {"gy": other}),
            remote(lane_send.at[t], lane_land.at[1, slot, t], 3, {"gx": mirror}),
        )

    def pack(acc, value, k):
        return jnp.where(lane // 2 == k, pltpu.roll(value, 2 * k + 1, 1), acc)

    def start_halo(slot, t):
        for copy in halo_copies(slot, t):
            copy.start()

    for f in range(1):
        for copy in gathers[: n_trc - 1]:
            copy.wait_recv()
        locals_[0].wait()
    first_label = me * tracers

    def begin(t, carry):
        label = first_label + t
        for r, start in enumerate(starts):
            acc = jnp.zeros((8, lanes), jnp.float32)
            for k in range(levels):
                wet = mk[k, start : start + 8, :].astype(jnp.float32)
                hit = col[k, start : start + 8, :] == label
                value = tr[t, k, start : start + 8, :] + pulse_height * jnp.where(hit, wet, 0.0)
                fx[0, t, k, OFF + start : OFF + start + 8, :] = value
                acc = pack(acc, value, k)
                if r == 0:
                    row_send[0, t, k : k + 1, :] = value[0:1, :]
                if r == tiles - 1:
                    row_send[1, t, k : k + 1, :] = value[7:8, :]
            lane_send[t, r] = acc
        start_halo(0, t)
        return carry

    lax.fori_loop(0, tracers, begin, 0)

    for copy in gathers[n_trc - 1 :]:
        copy.wait_recv()
    for copy in locals_[1:]:
        copy.wait()
    for copy in edges:
        copy.wait_recv()

    def coefficients(p, carry):
        for l in range(own):
            k = p * own + l
            for r, start in enumerate(starts):
                here = slice(start, start + 8)

                def westward(load, f):
                    if start:
                        return load(slice(start - 1, start + 7))
                    edge = west_land[p, f, l : l + 1, :]
                    return jnp.where(row == 0, edge, pltpu.roll(load(here), 1, 0))

                def field(f):
                    return lambda rows: ph[f, k, rows, :]

                def wetness(rows):
                    return mk[k, rows, :].astype(jnp.float32)

                wet = wetness(here)
                if r < tiles - 1:
                    wet_e = wetness(slice(start + 1, start + 9))
                else:
                    wet_e = jnp.where(row == 7, east_land[p, l : l + 1, :], pltpu.roll(wet, 7, 0))
                sides = side_land[p, r]

                def southward(value, f):
                    edge = pltpu.roll(sides, (lanes - 2 * (f * own + l)) % lanes, 1)
                    return jnp.where(lane == 0, edge, pltpu.roll(value, 1, 1))

                wet_n = jnp.where(
                    lane == lanes - 1,
                    jnp.where(is_top, 1.0, pltpu.roll(sides, lanes - 2 - 2 * (3 * own + l), 1)),
                    pltpu.roll(wet, lanes - 1, 1),
                )
                wet_s = southward(wet, 3)
                wet_s = jnp.where((lane == 0) & jnp.logical_not(is_top), 0.0, wet_s)
                speed, mix, slope = field(0)(here), field(2)(here), field(3)(here)

                def parts(speed, mix, slope, opened):
                    opened = time_step * opened
                    return (
                        (jnp.maximum(speed, 0.0) + mix) * opened,
                        (mix - jnp.minimum(speed, 0.0)) * opened,
                        (0.25 * mix * slope) * opened,
                    )

                ae, be, ce = parts(speed, mix, slope, wet * wet_e)
                aw, bw, cw = parts(
                    westward(field(0), 0), westward(field(2), 1), westward(field(3), 2),
                    wet * westward(wetness, 3),
                )
                speed, slope = field(1)(here), field(4)(here)
                an, bn, cn = parts(speed, mix, slope, wet * wet_n)
                a_s, bs, cs = parts(
                    southward(speed, 0), southward(mix, 1), southward(slope, 2), wet * wet_s
                )
                values = (
                    1.0 - ((ae + bw) + (an + bs)), be, aw, bn, a_s,
                    (ce - cw) + (cn - cs), ce, cw, cn, cs,
                )
                for c, value in enumerate(values):
                    coef[c, k, r] = value
        return carry

    lax.fori_loop(0, n_trc, coefficients, 0)

    def step(it, carry):
        s, t = it // tracers, lax.rem(it, tracers)
        now = lax.rem(s, 2)
        later = 1 - now
        for copy in halo_copies(now, t):
            copy.wait()
        from_east, from_west = row_land[0, now, t], row_land[1, now, t]
        for k in range(levels):
            fx[now, t, k, OFF - 1 : OFF, :] = from_west[k : k + 1, :]
            fx[now, t, k, OFF + columns : OFF + columns + 1, :] = from_east[k : k + 1, :]
        for r, start in enumerate(starts):
            near = lane_land[0, now, t, r]
            far = lane_land[1, now, t, tiles - 1 - r]
            for bit in (1, 2, 4):
                far = jnp.where((row & bit) == 0, pltpu.roll(far, 8 - bit, 0), pltpu.roll(far, bit, 0))
            upper = jnp.where((lane & 1) == 0, far, pltpu.roll(near, 1, 1))
            border = jnp.where(is_top, upper, pltpu.roll(near, lanes - 1, 1))
            at = OFF + start
            here, e, w, n, s_ = [], [], [], [], []
            for k in range(levels):
                f = fx[now, t, k, at : at + 8, :]
                here.append(f)
                e.append(fx[now, t, k, at + 1 : at + 9, :])
                w.append(fx[now, t, k, at - 1 : at + 7, :])
                ends = pltpu.roll(border, lanes - 1 - 2 * k, 1)
                n.append(jnp.where(lane == lanes - 1, ends, pltpu.roll(f, lanes - 1, 1)))
                s_.append(jnp.where(lane == 0, ends, pltpu.roll(f, 1, 1)))

            def dz(a, k):
                if k == 0:
                    return a[1]
                if k == levels - 1:
                    return -a[k - 1]
                return a[k + 1] - a[k - 1]

            acc = jnp.zeros((8, lanes), jnp.float32)
            for k in range(levels):
                c = [coef[i, k, r] for i in range(10)]
                value = (
                    (c[0] * here[k] + c[5] * dz(here, k))
                    + (c[1] * e[k] + c[6] * dz(e, k))
                    + (c[2] * w[k] - c[7] * dz(w, k))
                    + (c[3] * n[k] + c[8] * dz(n, k))
                    + (c[4] * s_[k] - c[9] * dz(s_, k))
                )
                fx[later, t, k, at : at + 8, :] = value
                acc = pack(acc, value, k)
                if r == 0:
                    row_send[0, t, k : k + 1, :] = value[0:1, :]
                if r == tiles - 1:
                    row_send[1, t, k : k + 1, :] = value[7:8, :]
            lane_send[t, r] = acc

        @pl.when(s < SUBSTEPS - 1)
        def _():
            start_halo(later, t)

        return carry

    lax.fori_loop(0, SUBSTEPS * tracers, step, 0)

    last = SUBSTEPS % 2

    def finish(t, carry):
        for k in range(levels):
            for start in starts:
                out[t, k, start : start + 8, :] = fx[last, t, k, OFF + start : OFF + start + 8, :]
        return carry

    lax.fori_loop(0, tracers, finish, 0)
    for copy in gathers + edges:
        copy.wait_send()


def local(n_trc, n_gx, *args):
    tracers, levels, columns, lanes = args[0].shape
    tiles = len(tile_starts(columns))
    f32 = jnp.float32
    vmem = pl.BlockSpec(memory_space=pltpu.VMEM)
    rows = -(-(OFF + columns + 1) // 8) * 8
    dma = pltpu.SemaphoreType.DMA
    return pl.pallas_call(
        functools.partial(kernel, n_trc, n_gx),
        out_shape=jax.ShapeDtypeStruct(args[0].shape, f32),
        in_specs=[vmem] * 8,
        out_specs=vmem,
        scratch_shapes=[
            pltpu.VMEM((5, levels, columns, lanes), f32),
            pltpu.VMEM((levels, columns, lanes), jnp.int32),
            pltpu.VMEM((4, 8, lanes), f32),
            pltpu.VMEM((8, lanes), f32),
            pltpu.VMEM((tiles, 8, lanes), f32),
            pltpu.VMEM((n_trc, 4, 8, lanes), f32),
            pltpu.VMEM((n_trc, 8, lanes), f32),
            pltpu.VMEM((n_trc, tiles, 8, lanes), f32),
            pltpu.VMEM((10, levels, tiles, 8, lanes), f32),
            pltpu.VMEM((2, tracers, levels, rows, lanes), f32),
            pltpu.VMEM((2, tracers, 8, lanes), f32),
            pltpu.VMEM((tracers, tiles, 8, lanes), f32),
            pltpu.VMEM((2, 2, tracers, 8, lanes), f32),
            pltpu.VMEM((2, 2, tracers, tiles, 8, lanes), f32),
            pltpu.VMEM((tiles, 8, lanes), f32),
            dma((6,)), dma((6, n_trc)), dma((6, n_trc)), dma((3, n_trc)), dma((3, n_trc)),
            dma((4, tracers)), dma((4, 2, tracers)),
        ],
        compiler_params=pltpu.CompilerParams(
            collective_id=0, has_side_effects=True, vmem_limit_bytes=40 * 1024 * 1024
        ),
    )(*args)


def solution(mesh):
    field = P("trc", "gx", "gy")
    in_specs = (P(("grp", "trc"), None, "gx", "gy"), P(None, "gx", "gy")) + (field,) * 6
    return jax.shard_map(
        functools.partial(local, mesh.shape["trc"], mesh.shape["gx"]),
        mesh=mesh, in_specs=in_specs, out_specs=in_specs[0], check_vma=False,
    )
```

```python
import functools

import jax
import jax.numpy as jnp
from jax import lax
from jax.experimental import pallas as pl
from jax.experimental.pallas import tpu as pltpu
from jax.sharding import PartitionSpec as P

SUBSTEPS = 4
time_step = 0.8
pulse_height = 1.0
MESH = pl.DeviceIdType.MESH


def kernel(
    n_trc, n_gx, group, tr, col, mask, u_in, v_in, m_in, se_in, sn_in, out,
    ph, big, west_edge, east_edge, side, west_land, east_land, side_land, shore,
    coef, rim, fx, lane_send, lane_land,
    gs_sem, gr_sem, fs_sem, fr_sem, es_sem, er_sem, hs_sem, hr_sem,
):
    tracers, columns, levels, lanes = tr.shape
    own = mask.shape[1]
    me, gx, gy, grp = (lax.axis_index(a) for a in ("trc", "gx", "gy", "grp"))
    east = lax.rem(gx + 1, n_gx)
    west = lax.rem(gx + n_gx - 1, n_gx)
    other, mirror, twin = 1 - gy, n_gx - 1 - gx, 1 - grp
    tile = (levels, lanes)
    lane = lax.broadcasted_iota(jnp.int32, tile, 1)
    row = lax.broadcasted_iota(jnp.int32, tile, 0)
    pair_of = lane // 2
    is_top = jnp.full(tile, gy, jnp.int32) == 1
    last = lanes - 1

    barrier = pltpu.get_barrier_semaphore()
    for d in range(n_trc):
        p = lax.rem(me + d, n_trc)
        if d:
            pl.semaphore_signal(barrier, inc=1, device_id={"trc": p}, device_id_type=MESH)
        for where in ({"trc": p, "gx": east}, {"trc": p, "gx": west}, {"trc": p, "gy": other}):
            pl.semaphore_signal(barrier, inc=1, device_id=where, device_id_type=MESH)
    pl.semaphore_signal(barrier, inc=1, device_id={"gx": mirror}, device_id_type=MESH)
    pl.semaphore_signal(barrier, inc=1, device_id={"grp": twin}, device_id_type=MESH)

    sources = (mask, m_in, u_in, v_in, se_in, sn_in)
    for f, ref in enumerate(sources):
        def stage(i, carry, f=f, ref=ref):
            ph[f, me, i] = ref[i].astype(jnp.float32)
            return carry

        lax.fori_loop(0, columns, stage, 0, unroll=True)
    for e, ref in enumerate((mask, m_in, u_in, se_in)):
        west_edge[e] = ref[columns - 1].astype(jnp.float32)
    east_edge[...] = mask[0].astype(jnp.float32)

    pl.semaphore_wait(barrier, 4 * n_trc + 1)

    def remote(src, dst, send, recv, where):
        return pltpu.make_async_remote_copy(
            src_ref=src, dst_ref=dst, send_sem=send, recv_sem=recv,
            device_id=where, device_id_type=MESH,
        )

    def gather(q, d):
        block = ph.at[2 * q + grp, me]
        return remote(
            block, block, gs_sem.at[q, d], gr_sem.at[q, d], {"trc": lax.rem(me + d, n_trc)}
        )

    def forward(q, d):
        block = ph.at[2 * q + grp, lax.rem(me + n_trc - d, n_trc)]
        return remote(block, block, fs_sem.at[q, d], fr_sem.at[q, d], {"grp": twin})

    others = range(1, n_trc)
    for q in range(3):
        for d in others:
            gather(q, d).start()

    half = lax.broadcasted_iota(jnp.int32, (own, lanes), 1) // 2
    for e, ref in enumerate((mask, m_in, v_in, sn_in)):
        acc = jnp.zeros((own, lanes), jnp.float32)
        for i in range(columns):
            value = ref[i].astype(jnp.float32)
            acc = jnp.where(half == i, pltpu.roll(value, 2 * i + 1, 1), acc)
        side[e] = acc
    edges = []
    for d in range(n_trc):
        p = lax.rem(me + d, n_trc)
        for e, (src, dst, where) in enumerate((
            (west_edge, west_land.at[me], {"trc": p, "gx": east}),
            (east_edge, east_land.at[me], {"trc": p, "gx": west}),
            (side, side_land.at[me], {"trc": p, "gy": other}),
        )):
            copy = remote(src, dst, es_sem.at[e, d], er_sem.at[e, d], where)
            copy.start()
            edges.append(copy)

    def halo_copies(slot, t):
        ts = pl.ds(t, group)

        def send(src, dst, e, where):
            return remote(src, dst, hs_sem.at[e, t], hr_sem.at[e, slot, t], where)

        return (
            send(fx.at[slot, ts, 1], fx.at[slot, ts, columns + 1], 0, {"gx": west}),
            send(fx.at[slot, ts, columns], fx.at[slot, ts, 0], 1, {"gx": east}),
            send(lane_send.at[0, ts], lane_land.at[0, slot, ts], 2, {"gy": other}),
            send(lane_send.at[1, ts], lane_land.at[1, slot, ts], 3, {"gx": mirror}),
        )

    def start_halo(slot, t):
        copies = halo_copies(slot, t)
        for copy in copies[:3]:
            copy.start()

        @pl.when(gy == 1)
        def _():
            copies[3].start()

    def wait_halo(slot, t):
        copies = halo_copies(slot, t)
        for copy in copies[:3]:
            copy.wait()

        @pl.when(gy == 1)
        def _():
            copies[3].wait()

    def pack(packs, value, i):
        near, far = packs
        near = jnp.where(pair_of == i, pltpu.roll(value, 2 * i + 1, 1), near)
        back = 2 * (columns - 1 - i)
        far = jnp.where(lane == back, pltpu.roll(value, back + 1, 1), far)
        return near, far

    def pass_on(q):
        for d in others:
            gather(q, d).wait_recv()
            forward(q, d).start()

    def assemble(f):
        for p in range(n_trc):
            def put(i, carry, p=p):
                big[f, i + 1, p * own : (p + 1) * own, :] = ph[f, p, i]
                return carry

            lax.fori_loop(0, columns, put, 0, unroll=True)

    pass_on(0)
    for d in others:
        forward(0, d).wait_recv()
    assemble(0)
    assemble(1)
    first_label = me * tracers
    zero = jnp.zeros(tile, jnp.float32)

    def begin(t):
        packs = [(zero, zero)] * group
        for i in range(columns):
            for a in range(group):
                hit = col[i] == first_label + (t + a)
                value = tr[t + a, i] + pulse_height * jnp.where(hit, big[0, i + 1], 0.0)
                fx[0, t + a, i + 1] = value
                packs[a] = pack(packs[a], value, i)
        for a in range(group):
            lane_send[0, t + a], lane_send[1, t + a] = packs[a]
        start_halo(0, t)

    batches = tracers // group
    for b in range(batches):
        begin(b * group)
        if b == 0:
            pass_on(1)
    pass_on(2)
    for copy in edges:
        copy.wait_recv()
    for e, f in enumerate((0, 1, 2, 4)):
        for p in range(n_trc):
            big[f, 0, p * own : (p + 1) * own, :] = west_land[p, e]
    for p in range(n_trc):
        big[0, columns + 1, p * own : (p + 1) * own, :] = east_land[p]
        for e in range(4):
            shore[e, p * own : (p + 1) * own, :] = side_land[p, e]
    for q in (1, 2):
        for d in others:
            forward(q, d).wait_recv()
        assemble(2 * q)
        assemble(2 * q + 1)

    def parts(speed, mix, slope, opened):
        opened = time_step * opened
        return (
            (jnp.maximum(speed, 0.0) + mix) * opened,
            (mix - jnp.minimum(speed, 0.0)) * opened,
            (0.25 * mix * slope) * opened,
        )

    def east_face(at):
        return parts(big[2, at], big[1, at], big[4, at], big[0, at] * big[0, at + 1])

    aw, bw, cw = east_face(0)
    rim_f, rim_z = zero, zero
    for i in range(columns):
        at = i + 1
        ae, be, ce = east_face(at)
        wet, mix, speed, slope = big[0, at], big[1, at], big[3, at], big[5, at]

        def southward(value, e):
            edge = pltpu.roll(shore[e], (lanes - 2 * i) % lanes, 1)
            return jnp.where(lane == 0, edge, pltpu.roll(value, 1, 1))

        above = jnp.where(is_top, 1.0, pltpu.roll(shore[0], (lanes - 2 - 2 * i) % lanes, 1))
        wet_n = jnp.where(lane == last, above, pltpu.roll(wet, last, 1))
        wet_s = jnp.where((lane > 0) | is_top, southward(wet, 0), 0.0)
        an, bn, cn = parts(speed, mix, slope, wet * wet_n)
        a_s, bs, cs = parts(
            southward(speed, 2), southward(mix, 1), southward(slope, 3), wet * wet_s
        )
        values = (
            1.0 - ((ae + bw) + (an + bs)), (ce - cw) + (cn - cs), be, ce, aw, cw,
            jnp.where(lane == last, 0.0, an), jnp.where(lane == last, 0.0, cn),
            jnp.where(lane == 0, 0.0, bs), jnp.where(lane == 0, 0.0, cs),
        )
        for c, value in enumerate(values):
            coef[c, i] = value
        here = pair_of == i
        rim_f = jnp.where(here, pltpu.roll(jnp.where(lane == last, bn, a_s), 2 * i + 1, 1), rim_f)
        rim_z = jnp.where(here, pltpu.roll(jnp.where(lane == last, cn, -cs), 2 * i + 1, 1), rim_z)
        aw, bw, cw = ae, be, ce
    rim[0], rim[1] = rim_f, rim_z

    def dz(f):
        upper = jnp.where(row < levels - 1, pltpu.roll(f, levels - 1, 0), 0.0)
        return upper - jnp.where(row > 0, pltpu.roll(f, 1, 0), 0.0)

    edge_lane = (lane == 0) | (lane == last)

    def step(it, carry):
        s, t = it // batches, lax.rem(it, batches) * group
        now = lax.rem(s, 2)
        later = 1 - now
        wait_halo(now, t)
        border, packs, window = [], [], []
        for a in range(group):
            near, far = lane_land[0, now, t + a], lane_land[1, now, t + a]
            upper = jnp.where((lane & 1) == 0, far, pltpu.roll(near, 1, 1))
            ends = jnp.where(is_top, upper, pltpu.roll(near, last, 1))
            border.append(rim[0] * ends + rim[1] * dz(ends))
            packs.append((zero, zero))
            f0, f1 = fx[now, t + a, 0], fx[now, t + a, 1]
            window.append((f0, dz(f0), f1, dz(f1)))
        for i in range(columns):
            c = [coef[x, i] for x in range(10)]
            for a in range(group):
                fw, zw, f, z = window[a]
                fe = fx[now, t + a, i + 2]
                ze = dz(fe)
                window[a] = (f, z, fe, ze)
                ends = pltpu.roll(border[a], (lanes - 1 - 2 * i) % lanes, 1)
                value = (
                    (c[0] * f + c[1] * z)
                    + (c[2] * fe + c[3] * ze)
                    + (c[4] * fw - c[5] * zw)
                    + (pltpu.roll(c[6] * f - c[7] * z, 1, 1) + pltpu.roll(c[8] * f + c[9] * z, last, 1))
                    + jnp.where(edge_lane, ends, 0.0)
                )
                fx[later, t + a, i + 1] = value
                packs[a] = pack(packs[a], value, i)
        for a in range(group):
            lane_send[0, t + a], lane_send[1, t + a] = packs[a]

        @pl.when(s < SUBSTEPS - 1)
        def _():
            start_halo(later, t)

        return carry

    lax.fori_loop(0, SUBSTEPS * batches, step, 0)

    final = SUBSTEPS % 2
    for t in range(tracers):
        for i in range(columns):
            out[t, i] = fx[final, t, i + 1]
    for copy in edges:
        copy.wait_send()
    for q in range(3):
        for d in others:
            gather(q, d).wait_send()
            forward(q, d).wait_send()


def local(n_trc, n_gx, tracers, colors, *fields):
    f32 = jnp.float32
    held = jnp.transpose(tracers, (0, 2, 1, 3))
    count, columns, levels, lanes = held.shape
    own = fields[0].shape[0]
    moved = [jnp.transpose(a, (1, 0, 2)) for a in (colors,) + fields]
    vmem = pl.BlockSpec(memory_space=pltpu.VMEM)
    dma = pltpu.SemaphoreType.DMA
    group = 2 if count % 2 == 0 else 1
    result = pl.pallas_call(
        functools.partial(kernel, n_trc, n_gx, group),
        out_shape=jax.ShapeDtypeStruct(held.shape, f32),
        in_specs=[vmem] * 8,
        out_specs=vmem,
        scratch_shapes=[
            pltpu.VMEM((6, n_trc, columns, own, lanes), f32),
            pltpu.VMEM((6, columns + 2, levels, lanes), f32),
            pltpu.VMEM((4, own, lanes), f32),
            pltpu.VMEM((own, lanes), f32),
            pltpu.VMEM((4, own, lanes), f32),
            pltpu.VMEM((n_trc, 4, own, lanes), f32),
            pltpu.VMEM((n_trc, own, lanes), f32),
            pltpu.VMEM((n_trc, 4, own, lanes), f32),
            pltpu.VMEM((4, levels, lanes), f32),
            pltpu.VMEM((10, columns, levels, lanes), f32),
            pltpu.VMEM((2, levels, lanes), f32),
            pltpu.VMEM((2, count, columns + 2, levels, lanes), f32),
            pltpu.VMEM((2, count, levels, lanes), f32),
            pltpu.VMEM((2, 2, count, levels, lanes), f32),
            dma((3, n_trc)), dma((3, n_trc)), dma((3, n_trc)), dma((3, n_trc)),
            dma((3, n_trc)), dma((3, n_trc)), dma((4, count)), dma((4, 2, count)),
        ],
        compiler_params=pltpu.CompilerParams(
            collective_id=0, has_side_effects=True, vmem_limit_bytes=40 * 1024 * 1024
        ),
    )(held, *moved)
    return jnp.transpose(result, (0, 2, 1, 3))


def solution(mesh):
    field = P("trc", "gx", "gy")
    in_specs = (P(("grp", "trc"), None, "gx", "gy"), P(None, "gx", "gy")) + (field,) * 6
    return jax.shard_map(
        functools.partial(local, mesh.shape["trc"], mesh.shape["gx"]),
        mesh=mesh, in_specs=in_specs, out_specs=in_specs[0], check_vma=False,
    )
```

```python
import functools

import jax
import jax.numpy as jnp
from jax import lax
from jax.experimental import pallas as pl
from jax.experimental.pallas import tpu as pltpu
from jax.sharding import PartitionSpec as P

SUBSTEPS = 4
time_step = 0.8
pulse_height = 1.0
MESH = pl.DeviceIdType.MESH


def kernel(
    n_trc, n_gx, group,
    tr_h, col_h, mask_h, u_h, v_h, m_h, se_h, sn_h, out,
    tr, col, mask, u_in, v_in, m_in, se_in, sn_in, in_sem,
    ph, big, west_edge, east_edge, side, west_land, east_land, side_land, shore,
    coef, rim, faces, bent, fx, lane_send, lane_land,
    gs_sem, gr_sem, fs_sem, fr_sem, es_sem, er_sem, hs_sem, hr_sem,
):
    tracers, columns, levels, lanes = tr.shape
    own = mask.shape[1]
    me, gx, gy, grp = (lax.axis_index(a) for a in ("trc", "gx", "gy", "grp"))
    east = lax.rem(gx + 1, n_gx)
    west = lax.rem(gx + n_gx - 1, n_gx)
    other, mirror, twin = 1 - gy, n_gx - 1 - gx, 1 - grp
    tile = (levels, lanes)
    lane = lax.broadcasted_iota(jnp.int32, tile, 1)
    row = lax.broadcasted_iota(jnp.int32, tile, 0)
    is_top = jnp.full(tile, gy, jnp.int32) == 1
    last = lanes - 1

    loads = [
        pltpu.make_async_copy(src, dst, in_sem.at[n])
        for n, (src, dst) in enumerate((
            (mask_h, mask), (m_h, m_in), (u_h, u_in), (v_h, v_in), (se_h, se_in), (sn_h, sn_in),
            (col_h, col), (tr_h, tr),
        ))
    ]
    for copy in loads:
        copy.start()

    barrier = pltpu.get_barrier_semaphore()
    for d in range(n_trc):
        p = lax.rem(me + d, n_trc)
        if d:
            pl.semaphore_signal(barrier, inc=1, device_id={"trc": p}, device_id_type=MESH)
        for where in ({"trc": p, "gx": east}, {"trc": p, "gx": west}, {"trc": p, "gy": other}):
            pl.semaphore_signal(barrier, inc=1, device_id=where, device_id_type=MESH)
    pl.semaphore_signal(barrier, inc=1, device_id={"gx": mirror}, device_id_type=MESH)
    pl.semaphore_signal(barrier, inc=1, device_id={"grp": twin}, device_id_type=MESH)

    for copy in loads[:6]:
        copy.wait()

    sources = (mask, m_in, u_in, v_in, se_in, sn_in)
    for f, ref in enumerate(sources):
        def stage(i, carry, f=f, ref=ref):
            ph[f, me, i] = ref[i].astype(jnp.float32)
            return carry

        lax.fori_loop(0, columns, stage, 0, unroll=True)
    for e, ref in enumerate((mask, m_in, u_in, se_in)):
        west_edge[e] = ref[columns - 1].astype(jnp.float32)
    east_edge[...] = mask[0].astype(jnp.float32)

    pl.semaphore_wait(barrier, 4 * n_trc + 1)

    def remote(src, dst, send, recv, where):
        return pltpu.make_async_remote_copy(
            src_ref=src, dst_ref=dst, send_sem=send, recv_sem=recv,
            device_id=where, device_id_type=MESH,
        )

    def gather(q, d):
        block = ph.at[2 * q + grp, me]
        return remote(
            block, block, gs_sem.at[q, d], gr_sem.at[q, d], {"trc": lax.rem(me + d, n_trc)}
        )

    def forward(q, d):
        block = ph.at[2 * q + grp, lax.rem(me + n_trc - d, n_trc)]
        return remote(block, block, fs_sem.at[q, d], fr_sem.at[q, d], {"grp": twin})

    others = range(1, n_trc)
    for q in range(3):
        for d in others:
            gather(q, d).start()

    half = lax.broadcasted_iota(jnp.int32, (own, lanes), 1) // 2
    for e, ref in enumerate((mask, m_in, v_in, sn_in)):
        acc = jnp.zeros((own, lanes), jnp.float32)
        for i in range(columns):
            value = ref[i].astype(jnp.float32)
            acc = jnp.where(half == i, pltpu.roll(value, 2 * i + 1, 1), acc)
        side[e] = acc
    edges = []
    for d in range(n_trc):
        p = lax.rem(me + d, n_trc)
        for e, (src, dst, where) in enumerate((
            (west_edge, west_land.at[me], {"trc": p, "gx": east}),
            (east_edge, east_land.at[me], {"trc": p, "gx": west}),
            (side, side_land.at[me], {"trc": p, "gy": other}),
        )):
            copy = remote(src, dst, es_sem.at[e, d], er_sem.at[e, d], where)
            copy.start()
            edges.append(copy)

    def tile_at(c, shift=0):
        return pl.ds(levels * (c + 1) + shift, levels)

    flat = faces.shape[1]
    ends_of = (((row == 0) & (lane == last)) | ((row == 1) & (lane == 0))).astype(jnp.float32)

    def edge_rows(value):
        return lax.dot_general(
            ends_of, value, (((1,), (1,)), ((), ())),
            precision=lax.Precision.HIGHEST, preferred_element_type=jnp.float32,
        )

    def pack(slot, t):
        body = [fx[slot, t, 2 * levels : (2 + columns) * levels, :]]
        if flat > columns * levels:
            body.append(fx[slot, t, 2 * levels : 2 * levels + flat - columns * levels, :])
        lane_send[0, t] = edge_rows(jnp.concatenate(body, axis=0))
        turned = [fx[slot, t, tile_at(columns - i), :] for i in range(columns)]
        turned += turned[:1] * (flat // levels - columns)
        lane_send[1, t] = edge_rows(jnp.concatenate(turned, axis=0))

    def halo_copies(slot, t):
        ts = pl.ds(t, group)

        def send(src, dst, e, where):
            return remote(src, dst, hs_sem.at[e, t], hr_sem.at[e, slot, t], where)

        return (
            send(fx.at[slot, ts, tile_at(1)], fx.at[slot, ts, tile_at(columns + 1)], 0, {"gx": west}),
            send(fx.at[slot, ts, tile_at(columns)], fx.at[slot, ts, tile_at(0)], 1, {"gx": east}),
            send(lane_send.at[0, ts], lane_land.at[0, slot, ts], 2, {"gy": other}),
            send(lane_send.at[1, ts], lane_land.at[1, slot, ts], 3, {"gx": mirror}),
        )

    def start_halo(slot, t):
        copies = halo_copies(slot, t)
        for copy in copies[:3]:
            copy.start()

        @pl.when(gy == 1)
        def _():
            copies[3].start()

    def wait_halo(slot, t):
        copies = halo_copies(slot, t)
        for copy in copies[:3]:
            copy.wait()

        @pl.when(gy == 1)
        def _():
            copies[3].wait()

    def pass_on(q):
        for d in others:
            gather(q, d).wait_recv()
            forward(q, d).start()

    def assemble(f):
        for p in range(n_trc):
            def put(i, carry, p=p):
                big[f, i + 1, p * own : (p + 1) * own, :] = ph[f, p, i]
                return carry

            lax.fori_loop(0, columns, put, 0, unroll=True)

    for copy in loads[6:]:
        copy.wait()
    pass_on(0)
    for d in others:
        forward(0, d).wait_recv()
    assemble(0)
    assemble(1)
    first_label = me * tracers

    def begin(t):
        for i in range(columns):
            for a in range(group):
                hit = col[i] == first_label + (t + a)
                value = tr[t + a, i] + pulse_height * jnp.where(hit, big[0, i + 1], 0.0)
                fx[0, t + a, tile_at(i + 1), :] = value
        for a in range(group):
            pack(0, t + a)
        start_halo(0, t)

    batches = tracers // group
    for b in range(batches):
        begin(b * group)
        if b == 0:
            pass_on(1)
    pass_on(2)
    for copy in edges:
        copy.wait_recv()
    for e, f in enumerate((0, 1, 2, 4)):
        for p in range(n_trc):
            big[f, 0, p * own : (p + 1) * own, :] = west_land[p, e]
    for p in range(n_trc):
        big[0, columns + 1, p * own : (p + 1) * own, :] = east_land[p]
        for e in range(4):
            shore[e, p * own : (p + 1) * own, :] = side_land[p, e]
    for q in (1, 2):
        for d in others:
            forward(q, d).wait_recv()
        assemble(2 * q)
        assemble(2 * q + 1)

    def parts(speed, mix, slope, opened):
        opened = time_step * opened
        return (
            (jnp.maximum(speed, 0.0) + mix) * opened,
            (mix - jnp.minimum(speed, 0.0)) * opened,
            (0.25 * mix * slope) * opened,
        )

    def east_face(at):
        return parts(big[2, at], big[1, at], big[4, at], big[0, at] * big[0, at + 1])

    aw, bw, cw = east_face(0)
    for i in range(columns):
        at = i + 1
        ae, be, ce = east_face(at)
        wet, mix, speed, slope = big[0, at], big[1, at], big[3, at], big[5, at]

        def southward(value, e):
            edge = pltpu.roll(shore[e], (lanes - 2 * i) % lanes, 1)
            return jnp.where(lane == 0, edge, pltpu.roll(value, 1, 1))

        above = jnp.where(is_top, 1.0, pltpu.roll(shore[0], (lanes - 2 - 2 * i) % lanes, 1))
        wet_n = jnp.where(lane == last, above, pltpu.roll(wet, last, 1))
        wet_s = jnp.where((lane > 0) | is_top, southward(wet, 0), 0.0)
        an, bn, cn = parts(speed, mix, slope, wet * wet_n)
        a_s, bs, cs = parts(
            southward(speed, 2), southward(mix, 1), southward(slope, 3), wet * wet_s
        )
        values = (
            1.0 - ((ae + bw) + (an + bs)), (ce - cw) + (cn - cs), be, ce, aw, cw,
            jnp.where(lane == last, 0.0, an), jnp.where(lane == last, 0.0, cn),
            jnp.where(lane == 0, 0.0, bs), jnp.where(lane == 0, 0.0, cs),
        )
        for c, value in enumerate(values):
            coef[c, i] = value
        faces[0, levels * i : levels * (i + 1), :] = jnp.where(lane == last, bn, a_s)
        faces[1, levels * i : levels * (i + 1), :] = jnp.where(lane == last, cn, -cs)
        aw, bw, cw = ae, be, ce
    for c in range(2):
        rim[c] = edge_rows(faces[c])

    flat_lane = lax.broadcasted_iota(jnp.int32, (8, flat), 1)
    flat_row = lax.broadcasted_iota(jnp.int32, (8, flat), 0)
    flat_level = lax.rem(flat_lane, levels)
    flat_top = jnp.full((8, flat), gy, jnp.int32) == 1

    def flat_dz(f):
        upper = jnp.where(flat_level < levels - 1, pltpu.roll(f, flat - 1, 1), 0.0)
        return upper - jnp.where(flat_level > 0, pltpu.roll(f, 1, 1), 0.0)

    def step(it, carry):
        s, t = it // batches, lax.rem(it, batches) * group
        now = lax.rem(s, 2)
        later = 1 - now
        wait_halo(now, t)

        def dz(a, c):
            upper = jnp.where(row < levels - 1, fx[now, t + a, tile_at(c, 1), :], 0.0)
            return upper - jnp.where(row > 0, fx[now, t + a, tile_at(c, -1), :], 0.0)

        window = []
        for a in range(group):
            near, far = lane_land[0, now, t + a], lane_land[1, now, t + a]
            upper = jnp.where(flat_row == 0, far, pltpu.roll(near, 1, 0))
            ends = jnp.where(flat_top, upper, pltpu.roll(near, 7, 0))
            ends = jnp.where(flat_row < 2, rim[0] * ends + rim[1] * flat_dz(ends), 0.0)
            bent[a] = lax.dot_general(
                ends, ends_of, (((0,), (0,)), ((), ())),
                precision=lax.Precision.HIGHEST, preferred_element_type=jnp.float32,
            )
            window.append((
                fx[now, t + a, tile_at(0), :], dz(a, 0), fx[now, t + a, tile_at(1), :], dz(a, 1)
            ))
        for i in range(columns):
            c = [coef[x, i] for x in range(10)]
            for a in range(group):
                fw, zw, f, z = window[a]
                fe = fx[now, t + a, tile_at(i + 2), :]
                ze = dz(a, i + 2)
                window[a] = (f, z, fe, ze)
                value = (
                    (c[0] * f + c[1] * z)
                    + (c[2] * fe + c[3] * ze)
                    + (c[4] * fw - c[5] * zw)
                    + (pltpu.roll(c[6] * f - c[7] * z, 1, 1) + pltpu.roll(c[8] * f + c[9] * z, last, 1))
                    + bent[a, levels * i : levels * (i + 1), :]
                )
                fx[later, t + a, tile_at(i + 1), :] = value

        @pl.when(s < SUBSTEPS - 1)
        def _():
            for a in range(group):
                pack(later, t + a)
            start_halo(later, t)

        return carry

    lax.fori_loop(0, SUBSTEPS * batches, step, 0)

    final = SUBSTEPS % 2
    for t in range(tracers):
        for i in range(columns):
            out[t, i] = fx[final, t, tile_at(i + 1), :]
    for copy in edges:
        copy.wait_send()
    for q in range(3):
        for d in others:
            gather(q, d).wait_send()
            forward(q, d).wait_send()


def local(n_trc, n_gx, tracers, colors, *fields):
    f32 = jnp.float32
    held = jnp.transpose(tracers, (0, 2, 1, 3))
    count, columns, levels, lanes = held.shape
    own = fields[0].shape[0]
    moved = [jnp.transpose(a, (1, 0, 2)) for a in (colors,) + fields]
    vmem = pl.BlockSpec(memory_space=pltpu.VMEM)
    dma = pltpu.SemaphoreType.DMA
    flat = -(-columns * levels // 128) * 128
    group = 2 if count % 2 == 0 else 1
    result = pl.pallas_call(
        functools.partial(kernel, n_trc, n_gx, group),
        out_shape=jax.ShapeDtypeStruct(held.shape, f32),
        in_specs=[pl.BlockSpec(memory_space=pltpu.HBM)] * 8,
        out_specs=vmem,
        scratch_shapes=[pltpu.VMEM(a.shape, a.dtype) for a in [held] + moved] + [
            dma((8,)),
            pltpu.VMEM((6, n_trc, columns, own, lanes), f32),
            pltpu.VMEM((6, columns + 2, levels, lanes), f32),
            pltpu.VMEM((4, own, lanes), f32),
            pltpu.VMEM((own, lanes), f32),
            pltpu.VMEM((4, own, lanes), f32),
            pltpu.VMEM((n_trc, 4, own, lanes), f32),
            pltpu.VMEM((n_trc, own, lanes), f32),
            pltpu.VMEM((n_trc, 4, own, lanes), f32),
            pltpu.VMEM((4, levels, lanes), f32),
            pltpu.VMEM((10, columns, levels, lanes), f32),
            pltpu.VMEM((2, 8, flat), f32),
            pltpu.VMEM((2, flat, lanes), f32),
            pltpu.VMEM((group, flat, lanes), f32),
            pltpu.VMEM((2, count, flat + 4 * levels, lanes), f32),
            pltpu.VMEM((2, count, 8, flat), f32),
            pltpu.VMEM((2, 2, count, 8, flat), f32),
            dma((3, n_trc)), dma((3, n_trc)), dma((3, n_trc)), dma((3, n_trc)),
            dma((3, n_trc)), dma((3, n_trc)), dma((4, count)), dma((4, 2, count)),
        ],
        compiler_params=pltpu.CompilerParams(
            collective_id=0, has_side_effects=True, vmem_limit_bytes=40 * 1024 * 1024
        ),
    )(held, *moved)
    return jnp.transpose(result, (0, 2, 1, 3))


def solution(mesh):
    field = P("trc", "gx", "gy")
    in_specs = (P(("grp", "trc"), None, "gx", "gy"), P(None, "gx", "gy")) + (field,) * 6
    return jax.shard_map(
        functools.partial(local, mesh.shape["trc"], mesh.shape["gx"]),
        mesh=mesh, in_specs=in_specs, out_specs=in_specs[0], check_vma=False,
    )
```
